768 devices in a mesh: seq: 48 (over x, z), dp: 16 (over y, core).
Axes of the slice: x: 4, y: 8, z: 12, core: 2. Of those that a mesh axis runs over, the one named last changes fastest.
Arguments:
- features: bfloat16 [16, 12288, 768], P('dp', 'seq'), may hold values from -6 to 6
- feature_cot: bfloat16 [16, 12288, 768], P('dp', 'seq'), may hold values from -6 to 6
- depth_weight: bfloat16 [3, 768], replicated, may hold values from -3.5 to 3.5
- mix_weight: bfloat16 [768, 768], replicated, may hold values from -0.21875 to 0.21875
- tissue_scale: bfloat16 [184, 768], replicated, may hold values from -12 to 12
- donor_site: int32 [16, 3072], P('dp', 'seq'), may hold values from 0 to 255
- acceptor_hop: int32 [16, 3072, 1], P('dp', 'seq'), may hold values from 0 to 4; in each aligned block of 64 rows (0 to 63, 64 to 127, ..., all dimensions but the last counted through in order) at most 16 rows name the same one
- acceptor_site: int32 [16, 3072], P('dp', 'seq'), may hold values from 0 to 255
- live_count: int32 [16, 48], P('dp', 'seq'), may hold values from 8 to 64, as said below
- score_cot: bfloat16 [16, 184, 3072], P('dp', None, 'seq'), may hold values from -6 to 6
Outputs:
- junction_scores: float32 [16, 184, 3072], P('dp', None, 'seq')
- input_grad: bfloat16 [16, 12288, 768], P('dp', 'seq')
- conv_grad: float32 [589824], P(('seq', 'dp'))
- scale_grads: float32 [143616], P(('seq', 'dp'))
The draws below stay inside these ranges and needn't reach their ends.
Inputs may be any that keep to these rules, and one draw needn't show every extreme that they name: Slots 0 to live_count - 1 of a shard hold junctions, the others are padding; in every sequence some shard has all 64 slots live. `acceptor_hop`: junctions whose acceptor shard falls outside the sequence are padding. Among the 64 slots of one shard no value occurs more than 16 times, and 16 is reached in some shard.
All inputs are finite; a program needn't handle non-finite values.
Results may differ from the reference program's by a relative error of at most 0.0083.
Values may be sent and summed in bfloat16 or wider, within the bound.
A program may use at most 32 MiB of HBM per device.

```python
import math
import jax
import jax.numpy as jnp
import numpy as np
from jax import lax

C = 768
TRACKS = 184
KW = 3
REACH = 2
LDEV = 256
JDEV = 64
CAP = 16
SHARDS = 48
L = 12288
NJ = 3072
B = 16


def draw_live_count(key, part):
    key = jax.random.fold_in(key, 11)
    key_shift, key_full = jax.random.split(key)
    halvings = jax.random.randint(key_shift, (B, SHARDS), 0, 4)
    counts = JDEV // jnp.left_shift(jnp.ones_like(halvings), halvings)
    fullest = jax.random.randint(key_full, (B, 1), 0, SHARDS)
    positions = jnp.arange(SHARDS, dtype=jnp.int32)[None, :]
    counts = jnp.where(positions == fullest, JDEV, counts)
    return counts.astype(jnp.int32)


def with_ends(result, rng, low, largest):
    longest = result.shape.index(max(result.shape))
    spots = []
    for shift in (0, 1):
        where = [jax.random.randint(jax.random.fold_in(rng, axis), (), 0, length) for axis, length in enumerate(result.shape)]
        where[longest] = (where[longest] + shift) % result.shape[longest]
        spots.append(tuple(where))
    return result.at[spots[0]].set(low).at[spots[1]].set(largest)


def block_levels(stream_key, extent, cuts, low, top_value):
    gain = 1.0
    for position, parts in cuts:
        draws = jax.random.uniform(jax.random.fold_in(jax.random.fold_in(stream_key, 6), position), (parts,), jnp.float32, low / len(cuts), top_value / len(cuts))
        gain = gain * jnp.repeat(jnp.exp(draws), extent[position] // parts).reshape((-1,) + (1,) * (len(extent) - 1 - position))
    return gain


def routed_block(stream_key, own, number, rows, amount, top, limit, lean):
    order = jax.random.permutation(stream_key, amount)
    packed, ordinary = shares(amount, rows * top, limit, lean, True), shares(amount, rows * top, limit, lean, False)
    places = jnp.arange(amount)

    def named(sizes, rotation):
        used = int((sizes > 0).sum())
        fixed = max(1, used // 4)
        shifted = fixed + (places - fixed + rotation * (used - fixed)) % max(1, amount - fixed)
        return jnp.zeros((amount,), jnp.int32).at[order[jnp.where(places < fixed, places, shifted)]].set(jnp.asarray(sizes, jnp.int32))

    sizes = jnp.where(number % 4 == 0, named(packed, number // 4), named(ordinary, number - number // 4 - 1))
    mixed = jax.random.permutation(jax.random.fold_in(own, 3), amount)
    donor, taker = mixed[0:amount // 2 * 2:2], mixed[1:amount // 2 * 2:2]
    margin = jnp.minimum(sizes[donor] - 1, limit - sizes[taker]) // 2
    margin = jnp.where((donor == order[0]) | (taker == order[0]) | (sizes[taker] == 0), 0, jnp.maximum(margin, 0))
    shifted = jax.random.randint(jax.random.fold_in(own, 4), (amount // 2,), 0, 1 << 20) % (margin + 1)
    sizes = sizes.at[donor].add(-shifted).at[taker].add(shifted)
    items = jnp.searchsorted(jnp.cumsum(sizes), jnp.arange(rows * top), side="right").astype(jnp.int32)
    grid = items.reshape(top, rows).T
    grid = grid[jax.random.permutation(jax.random.fold_in(own, 1), rows)]
    rotation = jax.random.randint(jax.random.fold_in(own, 2), (rows, 1), 0, top)
    return jnp.take_along_axis(grid, (jnp.arange(top)[None, :] + rotation) % top, axis=1)


def shares(amount, total, reach, lean, full):
    weights = [(1 << 20) // math.isqrt(grade ** lean) + 1 for grade in range(1, amount + 1)]
    largest = reach if full else min(reach, max(-(-total // amount), total * weights[0] // sum(weights)))
    least = 1 if total - largest >= amount - 1 else 0
    given, spare = [largest] + [least] * (amount - 1), total - largest - least * (amount - 1)
    while spare > 0:
        movable = [i for i in range(1, amount) if given[i] < largest] or [i for i in range(1, amount) if given[i] < reach]
        pool, left = sum([weights[i] for i in movable]), spare
        for i in movable:
            extra = min(reach - given[i], max(1, left * weights[i] // pool), spare)
            given[i] = given[i] + extra
            spare = spare - extra
    return np.array(given)


def bell_draw(key, extent, width, bound, cuts=(), held_as=jnp.bfloat16):
    gain = block_levels(key, extent, cuts, -0.22, 0.18) if cuts else 1.0
    entries = jax.random.normal(key, extent, jnp.float32) * width * gain
    return jnp.minimum(jnp.maximum(entries, -bound), bound).astype(held_as)


def setup_inputs(seed: int = 0) -> dict:
    seeds = jax.random.split(jax.random.key(seed), 11)
    features = bell_draw(seeds[0], (B, L, C), 1.0, 6.0, ((0, 16), (1, 48)))
    feature_cot = bell_draw(seeds[1], (B, L, C), 1.0, 6.0, ((0, 16), (1, 48)))
    depth_weight = bell_draw(seeds[2], (KW, C), KW ** -0.5, 3.5)
    mix_weight = bell_draw(seeds[3], (C, C), C ** -0.5, 0.21875)
    tissue_scale = bell_draw(seeds[4], (TRACKS, C), 2.0, 12.0)
    donor_site = with_ends(jax.random.randint(seeds[5], (B, NJ), 0, LDEV), jax.random.fold_in(seeds[5], 1), 0, LDEV - 1).astype(jnp.int32)
    acceptor_hop_keys = jax.random.split(jax.random.fold_in(seeds[6], 1), B * NJ // JDEV)
    acceptor_hop_turns = jax.random.permutation(jax.random.fold_in(seeds[6], 3), B * NJ // JDEV)
    acceptor_hop = jax.vmap(lambda own, number: routed_block(jax.random.fold_in(seeds[6], 2), own, number, JDEV, 2 * REACH + 1, 1, CAP, 2))(acceptor_hop_keys, acceptor_hop_turns).reshape((B, NJ, 1))
    acceptor_site = with_ends(jax.random.randint(seeds[7], (B, NJ), 0, LDEV), jax.random.fold_in(seeds[7], 1), 0, LDEV - 1).astype(jnp.int32)
    live_count = draw_live_count(jax.random.fold_in(seeds[10], 71), 0)
    score_cot = bell_draw(seeds[9], (B, TRACKS, NJ), 1.0, 6.0, ((0, 16), (2, 48)))
    return dict(features=features, feature_cot=feature_cot, depth_weight=depth_weight, mix_weight=mix_weight, tissue_scale=tissue_scale, donor_site=donor_site, acceptor_hop=acceptor_hop, acceptor_site=acceptor_site, live_count=live_count, score_cot=score_cot)


def pair_terms(donor_rows, acceptor_rows, cotangent, alive_mask, tissue_scale, inv_root):
    pair_product = (donor_rows.astype(jnp.float32) * acceptor_rows.astype(jnp.float32)).astype(jnp.bfloat16)
    raw_score = jnp.einsum('tc,mc->tm', tissue_scale.astype(jnp.float32), pair_product.astype(jnp.float32)) * inv_root
    alive_float = alive_mask.astype(jnp.float32)
    scores = jax.nn.softplus(raw_score) * alive_float
    score_slope = (cotangent.astype(jnp.float32) * jax.nn.sigmoid(raw_score) * alive_float).astype(jnp.bfloat16)
    track_mix = jnp.einsum('tm,tc->mc', score_slope.astype(jnp.float32), tissue_scale.astype(jnp.float32))
    return (pair_product, scores, score_slope, track_mix)

def reference(features, feature_cot, depth_weight, mix_weight, tissue_scale, donor_site, acceptor_hop, acceptor_site, live_count, score_cot):
    inv_root = 1.0 / math.sqrt(C)
    slot_ids = jnp.arange(NJ, dtype=jnp.int32)
    shard_ids = (slot_ids // JDEV).astype(jnp.int32)
    within = (slot_ids % JDEV).astype(jnp.int32)
    tap_count = depth_weight.shape[0]
    depth_float = depth_weight.astype(jnp.float32)

    def one_sequence(running, sequence_items):
        mix_total, tissue_total, depth_total = running
        inputs, upstream, donors, hops, acceptors, counts, cotangent = sequence_items
        padded = jnp.pad(inputs, ((1, 1), (0, 0)))
        smooth_acc = padded[0:L].astype(jnp.float32) * depth_float[0]
        for offset in range(1, tap_count):
            smooth_acc = smooth_acc + padded[offset:offset + L].astype(jnp.float32) * depth_float[offset]
        smoothed = smooth_acc.astype(jnp.bfloat16)
        pre_act = jnp.dot(smoothed, mix_weight, preferred_element_type=jnp.float32)
        activated, gelu_back = jax.vjp(jax.nn.gelu, pre_act)
        embedding = activated.astype(jnp.bfloat16)
        hop_values = hops[:, 0] - REACH
        target = shard_ids + hop_values
        slot_live = (within < counts[shard_ids]) & (target >= 0) & (target < SHARDS)
        donor_pos = (shard_ids * LDEV + donors).astype(jnp.int32)
        acceptor_pos = (jnp.clip(target, 0, SHARDS - 1) * LDEV + acceptors).astype(jnp.int32)
        donor_rows = embedding[donor_pos]
        acceptor_rows = embedding[acceptor_pos]
        pair_product, scores, score_slope, track_mix = pair_terms(donor_rows, acceptor_rows, cotangent, slot_live, tissue_scale, inv_root)
        live_column = slot_live.astype(jnp.float32)[:, None]
        grad_embed = upstream.astype(jnp.float32)
        grad_embed = grad_embed.at[acceptor_pos].add(track_mix * donor_rows.astype(jnp.float32) * inv_root * live_column)
        grad_embed = grad_embed.at[donor_pos].add(track_mix * acceptor_rows.astype(jnp.float32) * inv_root * live_column)
        pre_slope = gelu_back(grad_embed)[0].astype(jnp.bfloat16)
        smooth_slope = jnp.dot(pre_slope, mix_weight.T, preferred_element_type=jnp.float32).astype(jnp.bfloat16)
        padded_slope = jnp.pad(smooth_slope, ((1, 1), (0, 0)))
        input_grad = padded_slope[tap_count - 1:tap_count - 1 + L].astype(jnp.float32) * depth_float[0]
        for offset in range(1, tap_count):
            begin_row = tap_count - 1 - offset
            input_grad = input_grad + padded_slope[begin_row:begin_row + L].astype(jnp.float32) * depth_float[offset]
        slope_float = smooth_slope.astype(jnp.float32)
        depth_part = jnp.stack([lax.optimization_barrier(jnp.sum(padded[offset:offset + L].astype(jnp.float32) * slope_float, axis=0)) for offset in range(tap_count)])
        mix_part = jnp.dot(smoothed.T, pre_slope, preferred_element_type=jnp.float32)
        tissue_part = jnp.einsum('tm,mc->tc', score_slope.astype(jnp.float32), pair_product.astype(jnp.float32)) * inv_root
        return ((mix_total + mix_part, tissue_total + tissue_part, depth_total + depth_part), (scores, input_grad.astype(jnp.bfloat16)))
    initial = (jnp.zeros((C, C), jnp.float32), jnp.zeros((TRACKS, C), jnp.float32), jnp.zeros((KW, C), jnp.float32))
    totals, stacked = lax.scan(one_sequence, initial, (features, feature_cot, donor_site, acceptor_hop, acceptor_site, live_count, score_cot))
    mix_total, tissue_total, depth_total = totals
    junction_scores, input_grad = stacked
    grad_scale = 1.0 / math.sqrt(B * L)
    conv_grad = mix_total.reshape(-1) * grad_scale
    scale_grads = jnp.concatenate([tissue_total.reshape(-1), depth_total.reshape(-1) * grad_scale])
    return (junction_scores, input_grad, conv_grad, scale_grads)
```

```python
import math

import jax
import jax.numpy as jnp
from jax import lax
from jax.experimental import pallas as pl
from jax.experimental.pallas import tpu as pltpu
from jax.sharding import PartitionSpec as P

F32 = jnp.float32
BF16 = jnp.bfloat16
MESH = pl.DeviceIdType.MESH

REACH = 2
HOPS = 2 * REACH + 1
CAP = 16
NX, NZ, NY, NC = 4, 12, 8, 2
SHARDS = NX * NZ
ROWS = 256
CH = 768
HALF = CH // 2
TRACKS = 184
HEAD = TRACKS + 3
HEAD_PAD = 192
SLOTS = 64
BUCKET = HOPS * CAP
XROWS = CH // NX
TROWS = 48
ZROWS = XROWS // NZ
SHARE = HEAD * CH // (SHARDS * NY * NC)

S_CODE, S_ROWS, S_FEAT, S_SLOPE = 0, 5, 10, 12
S_SMOOTH, S_PRE, S_HEAD, S_END = 14, 15, 16, 17
S_XM, S_XT, S_Z, S_Y = 18, 21, 24, 35
S_ALL = 42


def dot(a, b, left=1, right=0):
    return lax.dot_general(
        a, b, (((left,), (right,)), ((), ())), preferred_element_type=F32
    )


def iota(shape, dim):
    return lax.broadcasted_iota(jnp.int32, shape, dim).astype(F32)


def quotient(value, divisor):
    return jnp.floor((value + 0.5) * (1.0 / divisor))


def body(
    feat,
    fcot,
    taps,
    mix,
    scale,
    donor,
    hop,
    acceptor,
    live,
    cot,
    scores_out,
    grad_out,
    conv_out,
    head_out,
    code_out,
    code_in,
    rows_out,
    rows_in,
    halo_in,
    edge_out,
    edge_in,
    fpad,
    spad,
    act,
    emb,
    smooth,
    smooth_in,
    pre,
    pre_in,
    head,
    head_cast,
    head_in,
    xm_out,
    xm_own,
    xm_in,
    xt_out,
    xt_in,
    z_out,
    z_in,
    y_out,
    y_in,
    end_out,
    end_in,
    send,
    recv,
):
    seq = lax.axis_index("seq")
    dp = lax.axis_index("dp")
    x, z = lax.div(seq, NZ), lax.rem(seq, NZ)
    y, core = lax.div(dp, NC), lax.rem(dp, NC)
    inv_root = 1.0 / math.sqrt(CH)
    grad_scale = 1.0 / math.sqrt(ROWS * SHARDS * NY * NC)

    def along_seq(step):
        return {"seq": lax.rem(seq + SHARDS + step, SHARDS), "dp": dp}

    def along_x(step):
        return {"seq": lax.rem(x + step, NX) * NZ + z, "dp": dp}

    def along_z(step):
        return {"seq": x * NZ + lax.rem(z + step, NZ), "dp": dp}

    def along_y(step):
        return {"seq": seq, "dp": lax.rem(y + step, NY) * NC + core}

    partner = {"seq": seq, "dp": y * NC + 1 - core}

    def remote(src, dst, number, device):
        return pltpu.make_async_remote_copy(
            src_ref=src,
            dst_ref=dst,
            send_sem=send.at[number],
            recv_sem=recv.at[number],
            device_id=device,
            device_id_type=MESH,
        )

    barrier = pltpu.get_barrier_semaphore()

    def greet(device):
        pl.semaphore_signal(barrier, inc=1, device_id=device, device_id_type=MESH)

    for step in (-2, -1, 1, 2):
        greet(along_seq(step))
    greet(partner)
    for step in range(1, NX):
        greet(along_x(step))

    @pl.loop(1, NZ)
    def _(step):
        greet(along_z(step))

    @pl.loop(1, NY)
    def _(step):
        greet(along_y(step))

    hop_row = hop[...].astype(F32)
    seq_f = seq.astype(F32)
    target = hop_row + (seq_f - REACH)
    slot_row = iota((1, SLOTS), 1)
    live_f = live[...].astype(F32)
    live_row = (slot_row < live_f) & (target >= 0.0) & (target < float(SHARDS))
    key_row = jnp.where(live_row, hop_row, 7.0)
    eye = iota((SLOTS, SLOTS), 0) == iota((SLOTS, SLOTS), 1)

    def column(row):
        return jnp.sum(jnp.where(eye, row, 0.0), axis=1, keepdims=True)

    key_col = column(key_row)
    before = iota((SLOTS, SLOTS), 0) < iota((SLOTS, SLOTS), 1)
    rank_row = jnp.sum(
        jnp.where((key_col == key_row) & before, 1.0, 0.0), axis=0, keepdims=True
    )
    rank_col = column(rank_row)
    place = iota((BUCKET, SLOTS), 0)
    place_hop = quotient(place, CAP)
    chosen = (key_row == place_hop) & (rank_row == place - CAP * place_hop)
    chosen = jnp.where(chosen, 1.0, 0.0).astype(BF16)
    place = iota((SLOTS, BUCKET), 1)
    place_hop = quotient(place, CAP)
    unchosen = (key_col == place_hop) & (rank_col == place - CAP * place_hop)
    unchosen = jnp.where(unchosen, 1.0, 0.0).astype(BF16)
    live_col = jnp.where(key_col < 6.0, 1.0, 0.0)
    donor_col = column(donor[...].astype(F32))
    donor_hot = jnp.where(
        (iota((SLOTS, ROWS), 1) == donor_col) & (key_col < 6.0), 1.0, 0.0
    ).astype(BF16)
    code_col = column(acceptor[...].astype(F32)) + 1.0
    code_wide = jnp.broadcast_to(code_col, (SLOTS, 128)).astype(BF16)
    bucket_cot = dot(chosen, cot[...])
    bucket_code = dot(chosen, code_wide)
    parcel = jnp.concatenate(
        [bucket_cot, jnp.zeros((BUCKET, 256 - TRACKS), F32), bucket_code], axis=1
    ).astype(BF16)
    for h in range(HOPS):
        code_out[h] = parcel[h * CAP : (h + 1) * CAP]
    code_in[REACH] = parcel[REACH * CAP : (REACH + 1) * CAP]
    bucket_hot = dot(chosen, donor_hot).astype(BF16)

    fpad[8 : 8 + ROWS, :] = feat[...].astype(F32)

    pl.semaphore_wait(barrier, 4 + 1 + (NX - 1) + (NZ - 1) + (NY - 1))

    others = [h for h in range(HOPS) if h != REACH]
    feat_right = remote(feat.at[pl.ds(ROWS - 16, 16)], halo_in.at[0], S_FEAT, along_seq(1))
    feat_left = remote(feat.at[pl.ds(0, 16)], halo_in.at[1], S_FEAT + 1, along_seq(-1))
    feat_right.start()
    feat_left.start()
    code_copies = [
        remote(code_out.at[h], code_in.at[h], S_CODE + h, along_seq(h - REACH)) for h in others
    ]
    for copy in code_copies:
        copy.start()

    feat_right.wait_recv()
    feat_left.wait_recv()
    inner_low = jnp.where(seq > 0, 1.0, 0.0)
    inner_high = jnp.where(seq < SHARDS - 1, 1.0, 0.0)
    fpad[0:8, :] = halo_in[0].astype(F32)[8:16] * inner_low
    fpad[8 + ROWS : 16 + ROWS, :] = halo_in[1].astype(F32)[0:8] * inner_high
    tap = [taps[k : k + 1, :].astype(F32) for k in range(3)]
    step_rows = 32
    for at in range(0, ROWS, step_rows):
        total = fpad[at + 7 : at + 7 + step_rows, :] * tap[0]
        total = total + fpad[at + 8 : at + 8 + step_rows, :] * tap[1]
        total = total + fpad[at + 9 : at + 9 + step_rows, :] * tap[2]
        emb[at : at + step_rows, :] = total.astype(BF16)
    smoothed = emb[...]
    act[...] = dot(smoothed, mix[...])
    turned = smoothed.T
    for k in range(NX):
        smooth[k] = turned[k * XROWS : (k + 1) * XROWS]
    smooth_copy = remote(smooth, smooth_in, S_SMOOTH, partner)
    smooth_copy.start()

    root = math.sqrt(2.0 / math.pi)

    @pl.loop(0, ROWS // step_rows)
    def _(i):
        at = pl.ds(pl.multiple_of(i * step_rows, step_rows), step_rows)
        v = act[at, :]
        sq = v * v
        t = jnp.tanh(root * (v + 0.044715 * (sq * v)))
        emb[at, :] = (0.5 * v * (1.0 + t)).astype(BF16)
        act[at, :] = 0.5 * (1.0 + t) + (0.5 * root) * v * (1.0 - t * t) * (
            1.0 + (3.0 * 0.044715) * sq
        )

    for copy in code_copies:
        copy.wait_recv()
    codes = code_in[...].reshape(BUCKET, 384)
    in_cot = codes[:, :TRACKS].astype(F32)
    in_code = codes[:, 256:384].astype(F32) - 1.0
    lanes = iota((BUCKET, 128), 1)
    in_hot = jnp.concatenate(
        [
            jnp.where(in_code == lanes, 1.0, 0.0),
            jnp.where(in_code == lanes + 128.0, 1.0, 0.0),
        ],
        axis=1,
    ).astype(BF16)
    hot = jnp.concatenate([in_hot, donor_hot, bucket_hot], axis=0)
    picked = dot(hot, emb[...]).astype(BF16)
    both = BUCKET + SLOTS
    own_rows = picked[:both]
    here = picked[:BUCKET]
    there = picked[both:]
    for h in range(HOPS):
        back = HOPS - 1 - h
        rows_out[h, 0:CAP, :] = there[h * CAP : (h + 1) * CAP]
        rows_out[h, CAP : 2 * CAP, :] = here[back * CAP : (back + 1) * CAP]
    rows_in[REACH] = rows_out[REACH]
    rows_copies = [
        remote(rows_out.at[h], rows_in.at[h], S_ROWS + h, along_seq(h - REACH)) for h in others
    ]
    for copy in rows_copies:
        copy.start()

    spread = hot[:both].T

    z_place = iota((XROWS, 3 * TROWS), 0)
    z_to = quotient(z_place, ZROWS)
    z_chunk = z_place - ZROWS * z_to
    z_tile = quotient(z_chunk, 5)
    x_f = x.astype(F32)
    z_f = z.astype(F32)
    x_base = quotient(jnp.full((1, 1), 187.0) * x_f, 4)
    z_row = quotient(187.0 * (NZ * x_f + z_to), 48) - x_base + (z_chunk - 5.0 * z_tile)
    z_pick = (iota((XROWS, 3 * TROWS), 1) == z_tile * TROWS + z_row) & (z_chunk < 15.0)
    z_pick = jnp.where(z_pick, 1.0, 0.0).astype(BF16)

    y_place = iota((NY * 16, 64), 0)
    y_to = quotient(y_place, 16)
    y_chunk = y_place - 16.0 * y_to
    y_half = jnp.where(y_chunk < 6.0, y_chunk, y_chunk - 6.0)
    y_second = jnp.where(y_half < 3.0, 0.0, 1.0)
    y_tile = y_half - 3.0 * y_second
    z_base = quotient(jnp.full((1, 1), 187.0) * seq_f, 48)
    y_row = quotient(187.0 * (NY * seq_f + y_to), 384) - z_base + y_second
    y_at = jnp.where(
        y_chunk < 6.0, 16.0 * y_tile + 2.0 * y_to + y_second, 48.0 + 5.0 * y_tile + y_row
    )
    y_there = (y_chunk < 6.0) | ((y_chunk < 12.0) & (y_row < 5.0))
    y_pick = (iota((NY * 16, 64), 1) == y_at) & y_there
    y_pick = jnp.where(y_pick, 1.0, 0.0).astype(BF16)

    for copy in rows_copies:
        copy.wait_recv()
    from_donor = jnp.concatenate([rows_in[h, 0:CAP, :] for h in range(HOPS)], axis=0)
    from_acceptor = jnp.concatenate(
        [rows_in[HOPS - 1 - h, CAP : 2 * CAP, :] for h in range(HOPS)], axis=0
    )
    other = jnp.concatenate([from_donor, dot(unchosen, from_acceptor).astype(BF16)], axis=0)
    other_f = other.astype(F32)
    pair = (own_rows.astype(F32) * other_f).astype(BF16)
    raw = dot(pair, scale[...], 1, 1) * inv_root
    small = jnp.exp(-jnp.abs(raw))
    sigmoid = jnp.where(raw >= 0.0, 1.0, small) / (1.0 + small)
    all_cot = jnp.concatenate([in_cot, cot[...].astype(F32) * live_col], axis=0)
    slope = (all_cot * sigmoid).astype(BF16)
    terms = dot(slope, scale[...]) * other_f * inv_root
    junction = dot(spread, terms.astype(BF16))
    for k in range(2):
        cols = slice(k * HALF, (k + 1) * HALF)
        total = fcot[:, cols].astype(F32) + junction[:, cols]
        pre[k] = (total * act[:, cols]).astype(BF16)
    pre_copy = remote(pre.at[1 - core], pre_in, S_PRE, partner)
    pre_copy.start()

    slope_s = dot(pre[0], mix[:, :HALF], 1, 1) + dot(pre[1], mix[:, HALF:], 1, 1)
    slope_s = slope_s.astype(BF16)
    spad[8 : 8 + ROWS, :] = slope_s.astype(F32)
    edge_out[0] = slope_s[ROWS - 16 :]
    edge_out[1] = slope_s[:16]
    edge_right = remote(edge_out.at[0], edge_in.at[0], S_SLOPE, along_seq(1))
    edge_left = remote(edge_out.at[1], edge_in.at[1], S_SLOPE + 1, along_seq(-1))
    edge_right.start()
    edge_left.start()

    tissue = dot(slope[BUCKET:].T, pair[BUCKET:]) * inv_root
    depth = []
    for k in range(3):
        part = jnp.zeros((1, CH), F32)
        for at in range(0, ROWS, step_rows):
            part = part + jnp.sum(
                fpad[at + 7 + k : at + 7 + k + step_rows, :]
                * spad[at + 8 : at + 8 + step_rows, :],
                axis=0,
                keepdims=True,
            )
        depth.append(part * grad_scale)
    depth = jnp.concatenate(depth + [jnp.zeros((5, CH), F32)], axis=0)
    for k in range(2):
        cols = slice(k * HALF, (k + 1) * HALF)
        head[k, 0:TRACKS, :] = tissue[:, cols]
        head[k, TRACKS:HEAD_PAD, :] = depth[:, cols]
        head_cast[k] = head[k].astype(BF16)
    head_copy = remote(head_cast.at[1 - core], head_in, S_HEAD, partner)
    head_copy.start()

    smooth_copy.wait_recv()
    pre_copy.wait_recv()
    pre_own = pre[core]
    pre_other = pre_in[...]
    xm_copies = {}
    for step in (2, 1, 3):
        to = lax.rem(x + step, NX)
        block = dot(smooth[to], pre_own) + dot(smooth_in[to], pre_other)
        xm_out[step - 1] = block.astype(BF16)
        xm_copies[step] = remote(
            xm_out.at[step - 1], xm_in.at[step - 1], S_XM + step - 1, along_x(step)
        )
        xm_copies[step].start()
    xm_own[...] = dot(smooth[x], pre_own) + dot(smooth_in[x], pre_other)

    head_copy.wait_recv()
    head[core] = head[core] + head_in[...].astype(F32)
    for k in range(NX):
        base = (187 * k) // 4
        xt_out[k] = head[core, base : base + TROWS, :].astype(BF16)
    xt_copies = {}
    for step in (2, 1, 3):
        to = lax.rem(x + step, NX)
        xt_copies[step] = remote(
            xt_out.at[to], xt_in.at[step - 1], S_XT + step - 1, along_x(step)
        )
        xt_copies[step].start()

    edge_right.wait_recv()
    edge_left.wait_recv()
    spad[0:8, :] = edge_in[0].astype(F32)[8:16] * inner_low
    spad[8 + ROWS : 16 + ROWS, :] = edge_in[1].astype(F32)[0:8] * inner_high
    for at in range(0, ROWS, step_rows):
        total = spad[at + 9 : at + 9 + step_rows, :] * tap[0]
        total = total + spad[at + 8 : at + 8 + step_rows, :] * tap[1]
        total = total + spad[at + 7 : at + 7 + step_rows, :] * tap[2]
        grad_out[at : at + step_rows, :] = total.astype(BF16)
    raw_d = raw[BUCKET:]
    softplus = jnp.maximum(raw_d, 0.0) + jnp.log1p(small[BUCKET:])
    scores_out[...] = softplus * live_col

    for step in range(1, NX):
        xm_copies[step].wait_recv()
    total = xm_own[...]
    for step in range(1, NX):
        total = total + xm_in[step - 1].astype(F32)
    for step in range(1, NX):
        xt_copies[step].wait_recv()
    tail = xt_out[x].astype(F32)
    for step in range(1, NX):
        tail = tail + xt_in[step - 1].astype(F32)
    tail = tail.astype(BF16)
    stacked = jnp.concatenate([tail[:, k * 128 : (k + 1) * 128] for k in range(3)], axis=0)
    chunks = dot(z_pick, stacked).astype(BF16)
    joined = jnp.concatenate([total.astype(BF16), chunks], axis=1)
    for k in range(NZ):
        z_out[k] = joined[k * ZROWS : (k + 1) * ZROWS]

    def z_copy(step):
        return remote(
            z_out.at[lax.rem(z + step, NZ)], z_in.at[step - 1], S_Z + step - 1, along_z(step)
        )

    @pl.loop(1, NZ)
    def _(step):
        z_copy(step).start()

    def z_add(step, total):
        z_copy(step).wait_recv()
        return total + z_in[step - 1].astype(F32)

    total = lax.fori_loop(1, NZ, z_add, z_out[z].astype(F32)).astype(BF16)
    stacked = jnp.concatenate([total[:, k * 128 : (k + 1) * 128] for k in range(4)], axis=0)
    chunks = dot(y_pick, stacked).astype(BF16)
    for k in range(NY):
        y_out[k] = chunks[k * 16 : (k + 1) * 16]

    def y_copy(step):
        return remote(
            y_out.at[lax.rem(y + step, NY)], y_in.at[step - 1], S_Y + step - 1, along_y(step)
        )

    @pl.loop(1, NY)
    def _(step):
        y_copy(step).start()

    def y_add(step, total):
        y_copy(step).wait_recv()
        return total + y_in[step - 1].astype(F32)

    total = lax.fori_loop(1, NY, y_add, y_out[y].astype(F32))

    end_out[...] = total
    end_copy = remote(end_out, end_in, S_END, partner)
    end_copy.start()
    end_copy.wait_recv()
    far = end_in[...]
    first = core == 0
    low = jnp.where(first, total, far)
    high = jnp.where(first, far, total)

    def strip(source, base):
        return [source[base + k : base + k + 1, :] for k in range(3)]

    row = [
        jnp.concatenate(strip(low, 3 * k) + strip(high, 3 * k), axis=1) for k in range(2)
    ]
    conv_out[...] = jnp.where(first, row[0], row[1]) * grad_scale
    line = jnp.concatenate(
        strip(low, 6) + strip(high, 6) + strip(low, 9) + strip(high, 9), axis=1
    )
    number = seq * NY + y
    begin = number * (2 * SHARE) - lax.div(number * (2 * SHARE), CH) * CH + core * SHARE
    line = jnp.broadcast_to(line, (8, 2 * CH))
    line = pltpu.roll(line, lax.rem(2 * CH - begin, 2 * CH), 1)
    head_out[...] = line[0:1, :SHARE]

    for copy in code_copies + rows_copies:
        copy.wait_send()
    for copy in (feat_right, feat_left, edge_right, edge_left):
        copy.wait_send()
    for copy in (smooth_copy, pre_copy, head_copy, end_copy):
        copy.wait_send()
    for step in range(1, NX):
        xm_copies[step].wait_send()
        xt_copies[step].wait_send()

    @pl.loop(1, NZ)
    def _(step):
        z_copy(step).wait_send()

    @pl.loop(1, NY)
    def _(step):
        y_copy(step).wait_send()


def on_device(
    features,
    feature_cot,
    depth_weight,
    mix_weight,
    tissue_scale,
    donor_site,
    acceptor_hop,
    acceptor_site,
    live_count,
    score_cot,
):
    vmem = pl.BlockSpec(memory_space=pltpu.VMEM)

    def room(*shape, dtype=BF16):
        return pltpu.VMEM(shape, dtype)

    scores, grad, conv, head = pl.pallas_call(
        body,
        out_shape=(
            jax.ShapeDtypeStruct((SLOTS, TRACKS), F32),
            jax.ShapeDtypeStruct((ROWS, CH), BF16),
            jax.ShapeDtypeStruct((1, CH), F32),
            jax.ShapeDtypeStruct((1, SHARE), F32),
        ),
        in_specs=[vmem] * 10,
        out_specs=(vmem,) * 4,
        scratch_shapes=[
            room(HOPS, CAP, 384),
            room(HOPS, CAP, 384),
            room(HOPS, 2 * CAP, CH),
            room(HOPS, 2 * CAP, CH),
            room(2, 16, CH),
            room(2, 16, CH),
            room(2, 16, CH),
            room(ROWS + 16, CH, dtype=F32),
            room(ROWS + 16, CH, dtype=F32),
            room(ROWS, CH, dtype=F32),
            room(ROWS, CH),
            room(NX, XROWS, ROWS),
            room(NX, XROWS, ROWS),
            room(2, ROWS, HALF),
            room(ROWS, HALF),
            room(2, HEAD_PAD, HALF, dtype=F32),
            room(2, HEAD_PAD, HALF),
            room(HEAD_PAD, HALF),
            room(NX - 1, XROWS, HALF),
            room(XROWS, HALF, dtype=F32),
            room(NX - 1, XROWS, HALF),
            room(NX, TROWS, HALF),
            room(NX - 1, TROWS, HALF),
            room(NZ, ZROWS, 512),
            room(NZ - 1, ZROWS, 512),
            room(NY, 16, 128),
            room(NY - 1, 16, 128),
            room(16, 128, dtype=F32),
            room(16, 128, dtype=F32),
            pltpu.SemaphoreType.DMA((S_ALL,)),
            pltpu.SemaphoreType.DMA((S_ALL,)),
        ],
        compiler_params=pltpu.CompilerParams(
            collective_id=0, has_side_effects=True, vmem_limit_bytes=40 * 1024 * 1024
        ),
    )(
        features[0],
        feature_cot[0],
        depth_weight,
        mix_weight,
        tissue_scale,
        donor_site,
        acceptor_hop.reshape(1, SLOTS),
        acceptor_site,
        live_count,
        score_cot[0].T,
    )
    return scores.T[None], grad[None], conv.reshape(CH), head.reshape(SHARE)


def solution(mesh):
    placed = (
        P("dp", "seq", None),
        P("dp", "seq", None),
        P(),
        P(),
        P(),
        P("dp", "seq"),
        P("dp", "seq", None),
        P("dp", "seq"),
        P("dp", "seq"),
        P("dp", None, "seq"),
    )
    return jax.shard_map(
        on_device,
        mesh=mesh,
        in_specs=placed,
        out_specs=(P("dp", None, "seq"), P("dp", "seq", None), P(("seq", "dp")), P(("seq", "dp"))),
        check_vma=False,
    )
```

```python
import math

import jax
import jax.numpy as jnp
from jax import lax
from jax.experimental import pallas as pl
from jax.experimental.pallas import tpu as pltpu
from jax.sharding import PartitionSpec as P

F32 = jnp.float32
BF16 = jnp.bfloat16
MESH = pl.DeviceIdType.MESH

REACH = 2
HOPS = 2 * REACH + 1
CAP = 16
NX, NZ, NY, NC = 4, 12, 8, 2
SHARDS = NX * NZ
DP = NY * NC
ROWS = 256
CH = 768
HALF = CH // 2
TRACKS = 184
HEAD = TRACKS + 3
HEAD_PAD = 192
SLOTS = 64
BUCKET = HOPS * CAP
XROWS = CH // NX
TROWS = 48
ZROWS = XROWS // NZ
SHARE = HEAD * CH // (SHARDS * NY * NC)

S_CODE, S_ROWS, S_FEAT, S_SLOPE = 0, 5, 10, 12
S_SMOOTH, S_PRE, S_HEAD = 14, 15, 16
S_XT, S_Z, S_Y = 20, 23, 34
S_T, S_TAPS, S_TAPS_X, S_TAPS_Z = 49, 60, 61, 64
S_XM = 75
S_ALL = 84

X_FAR, X_NEAR = (2, 1, 3), (1, 3, 2)
Z_FAR = (6, 5, 7, 4, 8, 3, 9, 2, 10, 1, 11)
PIECES = ((6, 5, 7, 4), (8, 3, 9, 2), (10, 1, 11, 0))
PROWS = ZROWS * len(PIECES[0])
D_FAR = (8, 7, 9, 6, 10, 5, 11, 4, 12, 3, 13, 2, 14, 1, 15)


def dot(a, b, left=1, right=0):
    return lax.dot_general(
        a, b, (((left,), (right,)), ((), ())), preferred_element_type=F32
    )


def iota(shape, dim):
    return lax.broadcasted_iota(jnp.int32, shape, dim).astype(F32)


def quotient(value, divisor):
    return jnp.floor((value + 0.5) * (1.0 / divisor))


def body(*refs):
    operands, targets, refs = refs[:10], refs[10:14], refs[14:]
    local, refs = refs[-1], refs[:-1]
    held, refs = refs[-10:], refs[:-10]
    loads = [
        pltpu.make_async_copy(src, dst, local.at[k])
        for k, (src, dst) in enumerate(zip(operands, held))
    ]
    for k in (0, 6, 8, 5, 7, 9, 2, 3, 4, 1):
        loads[k].start()
    stores = [
        pltpu.make_async_copy(src, dst, local.at[10 + k])
        for k, (src, dst) in enumerate(zip(refs[:4], targets))
    ]
    steps(loads, stores, *held, *refs)
    for copy in stores:
        copy.wait()


def steps(
    loads,
    stores,
    feat,
    fcot,
    taps,
    mix,
    scale,
    donor,
    hop,
    acceptor,
    live,
    cot,
    scores_out,
    grad_out,
    conv_out,
    head_out,
    code_out,
    code_in,
    rows_out,
    rows_in,
    halo_in,
    edge_out,
    edge_in,
    fpad,
    spad,
    act,
    emb,
    smooth,
    smooth_in,
    pre,
    pre_in,
    head,
    head_cast,
    head_in,
    xm_out,
    xm_own,
    xm_in,
    xt_out,
    xt_in,
    z_out,
    z_own,
    z_in,
    t_out,
    t_in,
    tail_sum,
    taps_part,
    taps_cast,
    taps_in,
    taps_sum,
    taps_out,
    taps_x,
    taps_z,
    d_out,
    d_in,
    send,
    recv,
):
    seq = lax.axis_index("seq")
    dp = lax.axis_index("dp")
    x, z = lax.div(seq, NZ), lax.rem(seq, NZ)
    y, core = lax.div(dp, NC), lax.rem(dp, NC)
    inv_root = 1.0 / math.sqrt(CH)
    grad_scale = 1.0 / math.sqrt(ROWS * SHARDS * NY * NC)

    def along_seq(step):
        return {"seq": lax.rem(seq + SHARDS + step, SHARDS), "dp": dp}

    def along_x(step):
        return {"seq": lax.rem(x + step, NX) * NZ + z, "dp": dp}

    def along_z(step):
        return {"seq": x * NZ + lax.rem(z + step, NZ), "dp": dp}

    def along_dp(step):
        return {"seq": seq, "dp": lax.rem(dp + step, DP)}

    partner = {"seq": seq, "dp": y * NC + 1 - core}

    def remote(src, dst, number, device):
        return pltpu.make_async_remote_copy(
            src_ref=src,
            dst_ref=dst,
            send_sem=send.at[number],
            recv_sem=recv.at[number],
            device_id=device,
            device_id_type=MESH,
        )

    leaving = []

    def start(copy):
        copy.start()
        leaving.append(copy)

    def done():
        for copy in leaving:
            copy.wait_send()

    barrier = pltpu.get_barrier_semaphore()

    def greet(device):
        pl.semaphore_signal(barrier, inc=1, device_id=device, device_id_type=MESH)

    for step in (-2, -1, 1, 2):
        greet(along_seq(step))
    for step in range(1, NX):
        greet(along_x(step))

    @pl.loop(1, NZ)
    def _(step):
        greet(along_z(step))

    @pl.loop(1, DP)
    def _(step):
        greet(along_dp(step))

    loads[0].wait()
    pl.semaphore_wait(barrier, 4 + (NX - 1) + (NZ - 1) + (DP - 1))

    feat_right = remote(feat.at[pl.ds(ROWS - 16, 16)], halo_in.at[0], S_FEAT, along_seq(1))
    feat_left = remote(feat.at[pl.ds(0, 16)], halo_in.at[1], S_FEAT + 1, along_seq(-1))
    start(feat_right)
    start(feat_left)

    for k in (5, 6, 7, 8, 9):
        loads[k].wait()

    hop_row = hop[...].astype(F32)
    seq_f = seq.astype(F32)
    target = hop_row + (seq_f - REACH)
    slot_row = iota((1, SLOTS), 1)
    live_f = live[...].astype(F32)
    live_row = (slot_row < live_f) & (target >= 0.0) & (target < float(SHARDS))
    key_row = jnp.where(live_row, hop_row, 7.0)
    eye = iota((SLOTS, SLOTS), 0) == iota((SLOTS, SLOTS), 1)

    def column(row):
        return jnp.sum(jnp.where(eye, row, 0.0), axis=1, keepdims=True)

    key_col = column(key_row)
    before = iota((SLOTS, SLOTS), 0) < iota((SLOTS, SLOTS), 1)
    rank_row = jnp.sum(
        jnp.where((key_col == key_row) & before, 1.0, 0.0), axis=0, keepdims=True
    )
    rank_col = column(rank_row)
    place = iota((BUCKET, SLOTS), 0)
    place_hop = quotient(place, CAP)
    chosen = (key_row == place_hop) & (rank_row == place - CAP * place_hop)
    chosen = jnp.where(chosen, 1.0, 0.0).astype(BF16)
    place = iota((SLOTS, BUCKET), 1)
    place_hop = quotient(place, CAP)
    unchosen = (key_col == place_hop) & (rank_col == place - CAP * place_hop)
    unchosen = jnp.where(unchosen, 1.0, 0.0).astype(BF16)
    live_col = jnp.where(key_col < 6.0, 1.0, 0.0)
    donor_col = column(donor[...].astype(F32))
    donor_hot = jnp.where(
        (iota((SLOTS, ROWS), 1) == donor_col) & (key_col < 6.0), 1.0, 0.0
    ).astype(BF16)
    code_col = column(acceptor[...].astype(F32)) + 1.0
    code_wide = jnp.broadcast_to(code_col, (SLOTS, 128)).astype(BF16)
    bucket_cot = dot(chosen, cot[...])
    bucket_code = dot(chosen, code_wide)
    parcel = jnp.concatenate(
        [bucket_cot, jnp.zeros((BUCKET, 256 - TRACKS), F32), bucket_code], axis=1
    ).astype(BF16)
    for h in range(HOPS):
        code_out[h] = parcel[h * CAP : (h + 1) * CAP]
    code_in[REACH] = parcel[REACH * CAP : (REACH + 1) * CAP]
    bucket_hot = dot(chosen, donor_hot).astype(BF16)

    fpad[8 : 8 + ROWS, :] = feat[...].astype(F32)

    others = [h for h in range(HOPS) if h != REACH]
    code_copies = [
        remote(code_out.at[h], code_in.at[h], S_CODE + h, along_seq(h - REACH)) for h in others
    ]
    for copy in code_copies:
        start(copy)

    for k in (1, 2, 3, 4):
        loads[k].wait()
    feat_right.wait_recv()
    feat_left.wait_recv()
    inner_low = jnp.where(seq > 0, 1.0, 0.0)
    inner_high = jnp.where(seq < SHARDS - 1, 1.0, 0.0)
    fpad[0:8, :] = halo_in[0].astype(F32)[8:16] * inner_low
    fpad[8 + ROWS : 16 + ROWS, :] = halo_in[1].astype(F32)[0:8] * inner_high
    tap = [taps[k : k + 1, :].astype(F32) for k in range(3)]
    step_rows = 32
    for at in range(0, ROWS, step_rows):
        total = fpad[at + 7 : at + 7 + step_rows, :] * tap[0]
        total = total + fpad[at + 8 : at + 8 + step_rows, :] * tap[1]
        total = total + fpad[at + 9 : at + 9 + step_rows, :] * tap[2]
        emb[at : at + step_rows, :] = total.astype(BF16)
    smoothed = emb[...]
    act[...] = dot(smoothed, mix[...])
    turned = smoothed.T
    for k in range(NX):
        for j in range(NZ):
            at = k * XROWS + j * ZROWS
            smooth[k, j] = turned[at : at + ZROWS]
    smooth_copy = remote(smooth, smooth_in, S_SMOOTH, partner)
    start(smooth_copy)

    root = math.sqrt(2.0 / math.pi)

    @pl.loop(0, ROWS // step_rows)
    def _(i):
        at = pl.ds(pl.multiple_of(i * step_rows, step_rows), step_rows)
        v = act[at, :]
        sq = v * v
        t = jnp.tanh(root * (v + 0.044715 * (sq * v)))
        emb[at, :] = (0.5 * v * (1.0 + t)).astype(BF16)
        act[at, :] = 0.5 * (1.0 + t) + (0.5 * root) * v * (1.0 - t * t) * (
            1.0 + (3.0 * 0.044715) * sq
        )

    for copy in code_copies:
        copy.wait_recv()
    codes = code_in[...].reshape(BUCKET, 384)
    in_cot = codes[:, :TRACKS].astype(F32)
    in_code = codes[:, 256:384].astype(F32) - 1.0
    lanes = iota((BUCKET, 128), 1)
    in_hot = jnp.concatenate(
        [
            jnp.where(in_code == lanes, 1.0, 0.0),
            jnp.where(in_code == lanes + 128.0, 1.0, 0.0),
        ],
        axis=1,
    ).astype(BF16)
    hot = jnp.concatenate([in_hot, donor_hot, bucket_hot], axis=0)
    picked = dot(hot, emb[...]).astype(BF16)
    both = BUCKET + SLOTS
    own_rows = picked[:both]
    here = picked[:BUCKET]
    there = picked[both:]
    for h in range(HOPS):
        back = HOPS - 1 - h
        rows_out[h, 0:CAP, :] = there[h * CAP : (h + 1) * CAP]
        rows_out[h, CAP : 2 * CAP, :] = here[back * CAP : (back + 1) * CAP]
    rows_in[REACH] = rows_out[REACH]
    rows_copies = [
        remote(rows_out.at[h], rows_in.at[h], S_ROWS + h, along_seq(h - REACH)) for h in others
    ]
    for copy in rows_copies:
        start(copy)

    spread = hot[:both].T

    z_place = iota((XROWS, 3 * TROWS), 0)
    z_to = quotient(z_place, ZROWS)
    z_chunk = z_place - ZROWS * z_to
    z_tile = quotient(z_chunk, 5)
    x_f = x.astype(F32)
    z_f = z.astype(F32)
    x_base = quotient(jnp.full((1, 1), 187.0) * x_f, 4)
    z_row = quotient(187.0 * (NZ * x_f + z_to), 48) - x_base + (z_chunk - 5.0 * z_tile)
    z_pick = (iota((XROWS, 3 * TROWS), 1) == z_tile * TROWS + z_row) & (z_chunk < 15.0)
    z_pick = jnp.where(z_pick, 1.0, 0.0).astype(BF16)

    d_place = iota((DP * 16, 64), 0)
    d_to = quotient(d_place, 16)
    d_chip = quotient(d_to, NC)
    d_chunk = d_place - 16.0 * d_to
    d_half = d_chunk - 3.0
    d_second = jnp.where(d_half < 3.0, 0.0, 1.0)
    d_tile = d_half - 3.0 * d_second
    z_base = quotient(jnp.full((1, 1), 187.0) * seq_f, 48)
    d_row = quotient(187.0 * (NY * seq_f + d_chip), 384) - z_base + d_second
    d_at = jnp.where(
        d_chunk < 3.0, 16.0 * d_chunk + d_to, 48.0 + 5.0 * d_tile + d_row
    )
    d_there = (d_chunk < 3.0) | ((d_chunk < 9.0) & (d_row < 5.0))
    d_pick = (iota((DP * 16, 64), 1) == d_at) & d_there
    d_pick = jnp.where(d_pick, 1.0, 0.0).astype(BF16)

    for copy in rows_copies:
        copy.wait_recv()
    from_donor = jnp.concatenate([rows_in[h, 0:CAP, :] for h in range(HOPS)], axis=0)
    from_acceptor = jnp.concatenate(
        [rows_in[HOPS - 1 - h, CAP : 2 * CAP, :] for h in range(HOPS)], axis=0
    )
    other = jnp.concatenate([from_donor, dot(unchosen, from_acceptor).astype(BF16)], axis=0)
    other_f = other.astype(F32)
    pair = (own_rows.astype(F32) * other_f).astype(BF16)
    raw = dot(pair, scale[...], 1, 1) * inv_root
    small = jnp.exp(-jnp.abs(raw))
    sigmoid = jnp.where(raw >= 0.0, 1.0, small) / (1.0 + small)
    all_cot = jnp.concatenate([in_cot, cot[...].astype(F32) * live_col], axis=0)
    slope = (all_cot * sigmoid).astype(BF16)
    tissue = dot(slope[BUCKET:].T, pair[BUCKET:]) * inv_root
    tissue = jnp.concatenate([tissue, jnp.zeros((HEAD_PAD - TRACKS, CH), F32)], axis=0)
    for k in range(2):
        head[k] = tissue[:, k * HALF : (k + 1) * HALF]
        head_cast[k] = head[k].astype(BF16)
    head_copy = remote(head_cast.at[1 - core], head_in, S_HEAD, partner)
    start(head_copy)
    terms = dot(slope, scale[...]) * other_f * inv_root
    junction = dot(spread, terms.astype(BF16))
    for k in range(2):
        cols = slice(k * HALF, (k + 1) * HALF)
        total = fcot[:, cols].astype(F32) + junction[:, cols]
        pre[k] = (total * act[:, cols]).astype(BF16)
    pre_copy = remote(pre.at[1 - core], pre_in, S_PRE, partner)
    start(pre_copy)

    head_copy.wait_recv()
    head[core] = head[core] + head_in[...].astype(F32)
    for k in range(NX):
        base = (187 * k) // 4
        xt_out[k] = head[core, base : base + TROWS, :].astype(BF16)
    xt_copies = {}
    for step in X_FAR:
        to = lax.rem(x + step, NX)
        xt_copies[step] = remote(
            xt_out.at[to], xt_in.at[step - 1], S_XT + step - 1, along_x(step)
        )
        start(xt_copies[step])

    smooth_copy.wait_recv()
    pre_copy.wait_recv()
    pre_own = pre[core]
    pre_other = pre_in[...]
    xm_copies = {}
    for n, piece in enumerate(PIECES):
        order = [lax.rem(x + step, NX) for step in (*X_FAR, 0)]
        parts = [
            jnp.concatenate(
                [source[to, lax.rem(z + step, NZ)] for to in order for step in piece], axis=0
            )
            for source in (smooth, smooth_in)
        ]
        block = dot(parts[0], pre_own) + dot(parts[1], pre_other)
        for k, step in enumerate(X_FAR):
            xm_out[n, step - 1] = block[k * PROWS : (k + 1) * PROWS].astype(BF16)
            copy = remote(
                xm_out.at[n, step - 1],
                xm_in.at[n, step - 1],
                S_XM + n * (NX - 1) + step - 1,
                along_x(step),
            )
            start(copy)
            xm_copies[n, step] = copy
        xm_own[n] = block[(NX - 1) * PROWS :]

    slope_s = dot(pre[0], mix[:, :HALF], 1, 1) + dot(pre[1], mix[:, HALF:], 1, 1)
    slope_s = slope_s.astype(BF16)
    spad[8 : 8 + ROWS, :] = slope_s.astype(F32)
    edge_out[0] = slope_s[ROWS - 16 :]
    edge_out[1] = slope_s[:16]
    edge_right = remote(edge_out.at[0], edge_in.at[0], S_SLOPE, along_seq(1))
    edge_left = remote(edge_out.at[1], edge_in.at[1], S_SLOPE + 1, along_seq(-1))
    start(edge_right)
    start(edge_left)

    for step in X_NEAR:
        xt_copies[step].wait_recv()
    tail = xt_out[x].astype(F32)
    for step in range(1, NX):
        tail = tail + xt_in[step - 1].astype(F32)
    tail = tail.astype(BF16)
    stacked = jnp.concatenate([tail[:, k * 128 : (k + 1) * 128] for k in range(3)], axis=0)
    chunks = dot(z_pick, stacked).astype(BF16)
    for k in range(NZ):
        t_out[k] = chunks[k * ZROWS : (k + 1) * ZROWS]

    def t_copy(step):
        return remote(
            t_out.at[lax.rem(z + step, NZ)], t_in.at[step - 1], S_T + step - 1, along_z(step)
        )

    t_copies = {step: t_copy(step) for step in range(1, NZ)}
    for step in Z_FAR:
        start(t_copies[step])

    z_copies = {}

    def pass_on(n):
        total = xm_own[n]
        for step in X_NEAR:
            xm_copies[n, step].wait_recv()
            total = total + xm_in[n, step - 1].astype(F32)
        for k, step in enumerate(PIECES[n]):
            rows = total[k * ZROWS : (k + 1) * ZROWS]
            if step == 0:
                z_own[...] = rows
                continue
            z_out[step - 1] = rows.astype(BF16)
            z_copies[step] = remote(
                z_out.at[step - 1], z_in.at[step - 1], S_Z + step - 1, along_z(step)
            )
            start(z_copies[step])

    pass_on(0)

    depth = []
    for k in range(3):
        part = jnp.zeros((1, CH), F32)
        for at in range(0, ROWS, step_rows):
            part = part + jnp.sum(
                fpad[at + 7 + k : at + 7 + k + step_rows, :]
                * spad[at + 8 : at + 8 + step_rows, :],
                axis=0,
                keepdims=True,
            )
        depth.append(part * grad_scale)
    for k in range(2):
        lines = [
            depth[tap_at][:, k * HALF + tile * 128 : k * HALF + tile * 128 + 128]
            for tile in range(3)
            for tap_at in range(3)
        ]
        total = jnp.concatenate(lines + [jnp.zeros((16 - 9, 128), F32)], axis=0)
        taps_part[k] = total
        taps_cast[k] = total.astype(BF16)
    taps_copy = remote(taps_cast.at[1 - core], taps_in, S_TAPS, partner)
    start(taps_copy)

    pass_on(1)

    taps_copy.wait_recv()
    taps_sum[...] = taps_part[core] + taps_in[...].astype(F32)
    last_x, last_z = x == NX - 1, (x == NX - 1) & (z == NZ - 1)

    def taps_to_x(source):
        return remote(
            taps_out,
            taps_x.at[source],
            S_TAPS_X + source,
            {"seq": (NX - 1) * NZ + z, "dp": dp},
        )

    def taps_to_z(source):
        return remote(
            taps_out,
            taps_z.at[source],
            S_TAPS_Z + source,
            {"seq": NX * NZ - 1, "dp": dp},
        )

    for source in range(NX - 1):

        @pl.when(x == source)
        def _():
            taps_out[...] = taps_sum[...].astype(BF16)
            taps_to_x(source).start()

    pass_on(2)

    @pl.when(last_x)
    def _():
        total = taps_sum[...]
        for source in range(NX - 1):
            taps_to_x(source).wait_recv()
            total = total + taps_x[source].astype(F32)
        taps_sum[...] = total
        taps_out[...] = total.astype(BF16)

    for source in range(NZ - 1):

        @pl.when(last_x & (z == source))
        def _():
            taps_to_z(source).start()

    edge_right.wait_recv()
    edge_left.wait_recv()
    spad[0:8, :] = edge_in[0].astype(F32)[8:16] * inner_low
    spad[8 + ROWS : 16 + ROWS, :] = edge_in[1].astype(F32)[0:8] * inner_high
    for at in range(0, ROWS, step_rows):
        total = spad[at + 9 : at + 9 + step_rows, :] * tap[0]
        total = total + spad[at + 8 : at + 8 + step_rows, :] * tap[1]
        total = total + spad[at + 7 : at + 7 + step_rows, :] * tap[2]
        grad_out[at : at + step_rows, :] = total.astype(BF16)
    raw_d = raw[BUCKET:]
    softplus = jnp.maximum(raw_d, 0.0) + jnp.log1p(small[BUCKET:])
    scores_out[...] = softplus * live_col
    stores[0].start()
    stores[1].start()

    tail = t_out[z].astype(F32)
    for step in Z_FAR[::-1]:
        t_copies[step].wait_recv()
        tail = tail + t_in[step - 1].astype(F32)
    tail_sum[...] = tail

    @pl.when(last_z)
    def _():
        total = taps_sum[...]
        for source in range(NZ - 1):
            taps_to_z(source).wait_recv()
            total = total + taps_z[source].astype(F32)
        for tile in range(3):
            at = 5 * tile + 1
            tail_sum[at : at + 3, :] = tail_sum[at : at + 3, :] + total[3 * tile : 3 * tile + 3]

    total = z_own[...]
    for step in Z_FAR[::-1]:
        z_copies[step].wait_recv()
        total = total + z_in[step - 1].astype(F32)
    total = jnp.concatenate([total, tail_sum[...]], axis=1).astype(BF16)
    stacked = jnp.concatenate([total[:, k * 128 : (k + 1) * 128] for k in range(4)], axis=0)
    chunks = dot(d_pick, stacked).astype(BF16)
    for k in range(DP):
        d_out[k] = chunks[k * 16 : (k + 1) * 16]

    def d_copy(step):
        return remote(
            d_out.at[lax.rem(dp + step, DP)], d_in.at[step - 1], S_Y + step - 1, along_dp(step)
        )

    d_copies = {step: d_copy(step) for step in range(1, DP)}
    for step in D_FAR:
        start(d_copies[step])
    sums = [d_out[dp].astype(F32), jnp.zeros((16, 128), F32)]
    for step in D_FAR[::-1]:
        d_copies[step].wait_recv()
        sums[step % 2] = sums[step % 2] + d_in[step - 1].astype(F32)

    first = core == 0
    low = jnp.where(first, sums[0], sums[1])
    high = jnp.where(first, sums[1], sums[0])

    def strip(source, base):
        return [source[base + k : base + k + 1, :] for k in range(3)]

    conv_out[...] = jnp.concatenate(strip(low, 0) + strip(high, 0), axis=1) * grad_scale
    stores[2].start()
    line = jnp.concatenate(
        strip(low, 3) + strip(high, 3) + strip(low, 6) + strip(high, 6), axis=1
    )
    number = seq * NY + y
    begin = number * (2 * SHARE) - lax.div(number * (2 * SHARE), CH) * CH + core * SHARE
    line = jnp.broadcast_to(line, (8, 2 * CH))
    line = pltpu.roll(line, lax.rem(2 * CH - begin, 2 * CH), 1)
    head_out[...] = line[0:1, :SHARE]
    stores[3].start()

    done()
    for source in range(NX - 1):

        @pl.when(x == source)
        def _():
            taps_to_x(source).wait_send()

    for source in range(NZ - 1):

        @pl.when(last_x & (z == source))
        def _():
            taps_to_z(source).wait_send()


def hand_over(*refs):
    sources, targets, held, sems = refs[:4], refs[4:8], refs[8:12], refs[12]
    loads = [
        pltpu.make_async_copy(src, dst, sems.at[k])
        for k, (src, dst) in enumerate(zip(sources, held))
    ]
    held = [held[0], held[1], held[2].at[0], held[3]]
    stores = [
        pltpu.make_async_copy(src, dst, sems.at[4 + k])
        for k, (src, dst) in enumerate(zip(held, targets))
    ]
    for copy in loads:
        copy.start()
    for load, store in zip(loads, stores):
        load.wait()
        store.start()
    for copy in stores:
        copy.wait()


def on_device(
    features,
    feature_cot,
    depth_weight,
    mix_weight,
    tissue_scale,
    donor_site,
    acceptor_hop,
    acceptor_site,
    live_count,
    score_cot,
):
    vmem = pl.BlockSpec(memory_space=pltpu.VMEM)
    hbm = pl.BlockSpec(memory_space=pltpu.HBM)

    def room(*shape, dtype=BF16):
        return pltpu.VMEM(shape, dtype)

    results = (
        jax.ShapeDtypeStruct((SLOTS, TRACKS), F32),
        jax.ShapeDtypeStruct((ROWS, CH), BF16),
        jax.ShapeDtypeStruct((1, CH), F32),
        jax.ShapeDtypeStruct((1, SHARE), F32),
    )
    made = pl.pallas_call(
        body,
        out_shape=results,
        in_specs=[hbm] * 10,
        out_specs=(hbm,) * 4,
        scratch_shapes=[
            room(SLOTS, TRACKS, dtype=F32),
            room(ROWS, CH),
            room(1, CH, dtype=F32),
            room(1, SHARE, dtype=F32),
            room(HOPS, CAP, 384),
            room(HOPS, CAP, 384),
            room(HOPS, 2 * CAP, CH),
            room(HOPS, 2 * CAP, CH),
            room(2, 16, CH),
            room(2, 16, CH),
            room(2, 16, CH),
            room(ROWS + 16, CH, dtype=F32),
            room(ROWS + 16, CH, dtype=F32),
            room(ROWS, CH, dtype=F32),
            room(ROWS, CH),
            room(NX, NZ, ZROWS, ROWS),
            room(NX, NZ, ZROWS, ROWS),
            room(2, ROWS, HALF),
            room(ROWS, HALF),
            room(2, HEAD_PAD, HALF, dtype=F32),
            room(2, HEAD_PAD, HALF),
            room(HEAD_PAD, HALF),
            room(len(PIECES), NX - 1, PROWS, HALF),
            room(len(PIECES), PROWS, HALF, dtype=F32),
            room(len(PIECES), NX - 1, PROWS, HALF),
            room(NX, TROWS, HALF),
            room(NX - 1, TROWS, HALF),
            room(NZ - 1, ZROWS, HALF),
            room(ZROWS, HALF, dtype=F32),
            room(NZ - 1, ZROWS, HALF),
            room(NZ, ZROWS, 128),
            room(NZ - 1, ZROWS, 128),
            room(16, 128, dtype=F32),
            room(2, 16, 128, dtype=F32),
            room(2, 16, 128),
            room(16, 128),
            room(16, 128, dtype=F32),
            room(16, 128),
            room(NX - 1, 16, 128),
            room(NZ - 1, 16, 128),
            room(DP, 16, 128),
            room(DP - 1, 16, 128),
            pltpu.SemaphoreType.DMA((S_ALL,)),
            pltpu.SemaphoreType.DMA((S_ALL,)),
            room(ROWS, CH),
            room(ROWS, CH),
            room(3, CH),
            room(CH, CH),
            room(TRACKS, CH),
            room(1, SLOTS, dtype=jnp.int32),
            room(1, SLOTS, dtype=jnp.int32),
            room(1, SLOTS, dtype=jnp.int32),
            room(1, 1, dtype=jnp.int32),
            room(SLOTS, TRACKS),
            pltpu.SemaphoreType.DMA((14,)),
        ],
        compiler_params=pltpu.CompilerParams(
            collective_id=0, has_side_effects=True, vmem_limit_bytes=63 * 1024 * 1024
        ),
    )(
        features[0],
        feature_cot[0],
        depth_weight,
        mix_weight,
        tissue_scale,
        donor_site,
        acceptor_hop.reshape(1, SLOTS),
        acceptor_site,
        live_count,
        score_cot[0].T,
    )
    scores, grad, conv, head = pl.pallas_call(
        hand_over,
        out_shape=results[:2] + (jax.ShapeDtypeStruct((CH,), F32), results[3]),
        in_specs=[hbm] * 4,
        out_specs=(hbm,) * 4,
        scratch_shapes=[
            room(SLOTS, TRACKS, dtype=F32),
            room(ROWS, CH),
            room(1, CH, dtype=F32),
            room(1, SHARE, dtype=F32),
            pltpu.SemaphoreType.DMA((8,)),
        ],
        compiler_params=pltpu.CompilerParams(vmem_limit_bytes=63 * 1024 * 1024),
    )(*made)
    return scores.T[None], grad[None], conv, head.reshape(SHARE)


def solution(mesh):
    placed = (
        P("dp", "seq", None),
        P("dp", "seq", None),
        P(),
        P(),
        P(),
        P("dp", "seq"),
        P("dp", "seq", None),
        P("dp", "seq"),
        P("dp", "seq"),
        P("dp", None, "seq"),
    )
    return jax.shard_map(
        on_device,
        mesh=mesh,
        in_specs=placed,
        out_specs=(P("dp", None, "seq"), P("dp", "seq", None), P(("seq", "dp")), P(("seq", "dp"))),
        check_vma=False,
    )
```

```python
import math

import jax
import jax.numpy as jnp
from jax import lax
from jax.experimental import pallas as pl
from jax.experimental.pallas import tpu as pltpu
from jax.sharding import PartitionSpec as P

F32 = jnp.float32
BF16 = jnp.bfloat16
MESH = pl.DeviceIdType.MESH

REACH = 2
HOPS = 2 * REACH + 1
CAP = 16
NX, NZ, NY, NC = 4, 12, 8, 2
SHARDS = NX * NZ
DP = NY * NC
ROWS = 256
CH = 768
HALF = CH // 2
TRACKS = 184
HEAD = TRACKS + 3
HEAD_PAD = 192
SLOTS = 64
BUCKET = HOPS * CAP
XROWS = CH // NX
TROWS = 48
ZROWS = XROWS // NZ
SHARE = HEAD * CH // (SHARDS * NY * NC)

S_CODE, S_ROWS, S_FEAT, S_SLOPE = 0, 5, 10, 12
S_SMOOTH, S_PRE, S_HEAD = 14, 15, 16
S_XT, S_Z, S_Y = 20, 23, 34
S_T, S_TAPS, S_TAPS_X, S_TAPS_Z = 49, 60, 61, 64
S_XM = 75
S_ALL = 84

X_FAR, X_NEAR = (2, 1, 3), (1, 3, 2)
Z_FAR = (6, 5, 7, 4, 8, 3, 9, 2, 10, 1, 11)
PIECES = ((6, 5, 7, 4), (8, 3, 9, 2), (10, 1, 11, 0))
PROWS = ZROWS * len(PIECES[0])
D_FAR = (8, 7, 9, 6, 10, 5, 11, 4, 12, 3, 13, 2, 14, 1, 15)


def dot(a, b, left=1, right=0):
    return lax.dot_general(
        a, b, (((left,), (right,)), ((), ())), preferred_element_type=F32
    )


def iota(shape, dim):
    return lax.broadcasted_iota(jnp.int32, shape, dim).astype(F32)


def wrapped(value, size):
    value = jnp.where(value < 0, value + size, value)
    return jnp.where(value >= size, value - size, value)


def quotient(value, divisor):
    return jnp.floor((value + 0.5) * (1.0 / divisor))


def body(*refs):
    operands, targets, refs = refs[:10], refs[10:14], refs[14:]
    local, refs = refs[-1], refs[:-1]
    held, refs = refs[-10:], refs[:-10]
    loads = [
        pltpu.make_async_copy(src, dst, local.at[k])
        for k, (src, dst) in enumerate(zip(operands, held))
    ]
    for k in (0, 6, 8, 5, 7, 9, 2, 3, 4, 1):
        loads[k].start()
    stores = [
        pltpu.make_async_copy(src, dst, local.at[10 + k])
        for k, (src, dst) in enumerate(zip(refs[:4], targets))
    ]
    steps(loads, stores, *held, *refs)
    for copy in stores:
        copy.wait()


def steps(
    loads,
    stores,
    feat,
    fcot,
    taps,
    mix,
    scale,
    donor,
    hop,
    acceptor,
    live,
    cot,
    scores_out,
    grad_out,
    conv_out,
    head_out,
    code_out,
    code_in,
    rows_out,
    rows_in,
    halo_in,
    edge_out,
    edge_in,
    fpad,
    spad,
    act,
    bend,
    smooth_held,
    emb,
    smooth,
    smooth_in,
    pre,
    pre_in,
    head,
    head_cast,
    head_in,
    xm_out,
    xm_own,
    xm_in,
    xt_out,
    xt_in,
    z_out,
    z_own,
    z_in,
    t_out,
    t_in,
    tail_sum,
    taps_part,
    taps_cast,
    taps_in,
    taps_sum,
    taps_out,
    taps_x,
    taps_z,
    d_out,
    d_in,
    send,
    recv,
):
    seq = lax.axis_index("seq")
    dp = lax.axis_index("dp")
    x, z = lax.div(seq, NZ), lax.rem(seq, NZ)
    y, core = lax.div(dp, NC), lax.rem(dp, NC)
    inv_root = 1.0 / math.sqrt(CH)
    grad_scale = 1.0 / math.sqrt(ROWS * SHARDS * NY * NC)

    def along_seq(step):
        return {"seq": wrapped(seq + step, SHARDS), "dp": dp}

    def along_x(step):
        return {"seq": wrapped(x + step, NX) * NZ + z, "dp": dp}

    def along_z(step):
        return {"seq": x * NZ + wrapped(z + step, NZ), "dp": dp}

    def along_dp(step):
        return {"seq": seq, "dp": wrapped(dp + step, DP)}

    partner = {"seq": seq, "dp": y * NC + 1 - core}

    def remote(src, dst, number, device):
        return pltpu.make_async_remote_copy(
            src_ref=src,
            dst_ref=dst,
            send_sem=send.at[number],
            recv_sem=recv.at[number],
            device_id=device,
            device_id_type=MESH,
        )

    leaving = []

    def start(copy):
        copy.start()
        leaving.append(copy)

    def done():
        for copy in leaving:
            copy.wait_send()

    barrier = pltpu.get_barrier_semaphore()

    def greet(device):
        pl.semaphore_signal(barrier, inc=1, device_id=device, device_id_type=MESH)

    for step in (-2, -1, 1, 2):
        greet(along_seq(step))
    for step in range(1, NX):
        greet(along_x(step))

    for step in range(1, NZ):
        greet(along_z(step))
    for step in range(1, DP):
        greet(along_dp(step))

    loads[0].wait()
    pl.semaphore_wait(barrier, 4 + (NX - 1) + (NZ - 1) + (DP - 1))

    feat_right = remote(feat.at[pl.ds(ROWS - 16, 16)], halo_in.at[0], S_FEAT, along_seq(1))
    feat_left = remote(feat.at[pl.ds(0, 16)], halo_in.at[1], S_FEAT + 1, along_seq(-1))
    start(feat_right)
    start(feat_left)

    for k in (5, 6, 7, 8, 9):
        loads[k].wait()

    hop_row = hop[...].astype(F32)
    seq_f = seq.astype(F32)
    target = hop_row + (seq_f - REACH)
    slot_row = iota((1, SLOTS), 1)
    live_f = live[...].astype(F32)
    live_row = (slot_row < live_f) & (target >= 0.0) & (target < float(SHARDS))
    key_row = jnp.where(live_row, hop_row, 7.0)
    eye = iota((SLOTS, SLOTS), 0) == iota((SLOTS, SLOTS), 1)

    def column(row):
        return jnp.sum(jnp.where(eye, row, 0.0), axis=1, keepdims=True)

    key_col = column(key_row)
    before = iota((SLOTS, SLOTS), 0) < iota((SLOTS, SLOTS), 1)
    rank_row = jnp.sum(
        jnp.where((key_col == key_row) & before, 1.0, 0.0), axis=0, keepdims=True
    )
    rank_col = column(rank_row)
    place = iota((BUCKET, SLOTS), 0)
    place_hop = quotient(place, CAP)
    chosen = (key_row == place_hop) & (rank_row == place - CAP * place_hop)
    chosen = jnp.where(chosen, 1.0, 0.0).astype(BF16)
    place = iota((SLOTS, BUCKET), 1)
    place_hop = quotient(place, CAP)
    unchosen = (key_col == place_hop) & (rank_col == place - CAP * place_hop)
    unchosen = jnp.where(unchosen, 1.0, 0.0).astype(BF16)
    live_col = jnp.where(key_col < 6.0, 1.0, 0.0)
    donor_col = column(donor[...].astype(F32))
    donor_hot = jnp.where(
        (iota((SLOTS, ROWS), 1) == donor_col) & (key_col < 6.0), 1.0, 0.0
    ).astype(BF16)
    code_col = column(acceptor[...].astype(F32)) + 1.0
    code_wide = jnp.broadcast_to(code_col, (SLOTS, 128)).astype(BF16)
    bucket_cot = dot(chosen, cot[...])
    bucket_code = dot(chosen, code_wide)
    parcel = jnp.concatenate(
        [bucket_cot, jnp.zeros((BUCKET, 256 - TRACKS), F32), bucket_code], axis=1
    ).astype(BF16)
    for h in range(HOPS):
        code_out[h] = parcel[h * CAP : (h + 1) * CAP]
    code_in[REACH] = parcel[REACH * CAP : (REACH + 1) * CAP]
    bucket_hot = dot(chosen, donor_hot).astype(BF16)

    fpad[8 : 8 + ROWS, :] = feat[...].astype(F32)

    others = [h for h in range(HOPS) if h != REACH]
    code_copies = [
        remote(code_out.at[h], code_in.at[h], S_CODE + h, along_seq(h - REACH)) for h in others
    ]
    for copy in code_copies:
        start(copy)

    z_place = iota((XROWS, 3 * TROWS), 0)
    z_to = quotient(z_place, ZROWS)
    z_chunk = z_place - ZROWS * z_to
    z_tile = quotient(z_chunk, 5)
    x_f = x.astype(F32)
    z_f = z.astype(F32)
    x_base = quotient(jnp.full((1, 1), 187.0) * x_f, 4)
    z_row = quotient(187.0 * (NZ * x_f + z_to), 48) - x_base + (z_chunk - 5.0 * z_tile)
    z_pick = (iota((XROWS, 3 * TROWS), 1) == z_tile * TROWS + z_row) & (z_chunk < 15.0)
    z_pick = jnp.where(z_pick, 1.0, 0.0).astype(BF16)

    d_place = iota((DP * 16, 64), 0)
    d_to = quotient(d_place, 16)
    d_chip = quotient(d_to, NC)
    d_chunk = d_place - 16.0 * d_to
    d_half = d_chunk - 3.0
    d_second = jnp.where(d_half < 3.0, 0.0, 1.0)
    d_tile = d_half - 3.0 * d_second
    z_base = quotient(jnp.full((1, 1), 187.0) * seq_f, 48)
    d_row = quotient(187.0 * (NY * seq_f + d_chip), 384) - z_base + d_second
    d_at = jnp.where(
        d_chunk < 3.0, 16.0 * d_chunk + d_to, 48.0 + 5.0 * d_tile + d_row
    )
    d_there = (d_chunk < 3.0) | ((d_chunk < 9.0) & (d_row < 5.0))
    d_pick = (iota((DP * 16, 64), 1) == d_at) & d_there
    d_pick = jnp.where(d_pick, 1.0, 0.0).astype(BF16)

    for k in (1, 2, 3, 4):
        loads[k].wait()
    feat_right.wait_recv()
    feat_left.wait_recv()
    inner_low = jnp.where(seq > 0, 1.0, 0.0)
    inner_high = jnp.where(seq < SHARDS - 1, 1.0, 0.0)
    fpad[0:8, :] = halo_in[0].astype(F32)[8:16] * inner_low
    fpad[8 + ROWS : 16 + ROWS, :] = halo_in[1].astype(F32)[0:8] * inner_high
    tap = [taps[k : k + 1, :].astype(F32) for k in range(3)]
    step_rows = 32
    for at in range(0, ROWS, step_rows):
        total = fpad[at + 7 : at + 7 + step_rows, :] * tap[0]
        total = total + fpad[at + 8 : at + 8 + step_rows, :] * tap[1]
        total = total + fpad[at + 9 : at + 9 + step_rows, :] * tap[2]
        smooth_held[at : at + step_rows, :] = total.astype(BF16)
    act[...] = dot(smooth_held[...], mix[...])
    root = math.sqrt(2.0 / math.pi)

    @pl.loop(0, ROWS // step_rows)
    def _(i):
        at = pl.ds(pl.multiple_of(i * step_rows, step_rows), step_rows)
        v = act[at, :]
        t = jnp.tanh(root * (v + 0.044715 * (v * v * v)))
        bend[at, :] = t
        emb[at, :] = (0.5 * v * (1.0 + t)).astype(BF16)

    for copy in code_copies:
        copy.wait_recv()
    codes = code_in[...].reshape(BUCKET, 384)
    in_cot = codes[:, :TRACKS].astype(F32)
    in_code = codes[:, 256:384].astype(F32) - 1.0
    lanes = iota((BUCKET, 128), 1)
    in_hot = jnp.concatenate(
        [
            jnp.where(in_code == lanes, 1.0, 0.0),
            jnp.where(in_code == lanes + 128.0, 1.0, 0.0),
        ],
        axis=1,
    ).astype(BF16)
    hot = jnp.concatenate([in_hot, donor_hot, bucket_hot], axis=0)
    picked = dot(hot, emb[...]).astype(BF16)
    both = BUCKET + SLOTS
    own_rows = picked[:both]
    here = picked[:BUCKET]
    there = picked[both:]
    for h in range(HOPS):
        back = HOPS - 1 - h
        rows_out[h, 0:CAP, :] = there[h * CAP : (h + 1) * CAP]
        rows_out[h, CAP : 2 * CAP, :] = here[back * CAP : (back + 1) * CAP]
    rows_in[REACH] = rows_out[REACH]
    rows_copies = [
        remote(rows_out.at[h], rows_in.at[h], S_ROWS + h, along_seq(h - REACH)) for h in others
    ]
    for copy in rows_copies:
        start(copy)

    spread = hot[:both].T
    turned = smooth_held[...].T
    for k in range(NX):
        for j in range(NZ):
            at = k * XROWS + j * ZROWS
            smooth[k, j] = turned[at : at + ZROWS]
    smooth_copy = remote(smooth, smooth_in, S_SMOOTH, partner)
    start(smooth_copy)


    @pl.loop(0, ROWS // step_rows)
    def _(i):
        at = pl.ds(pl.multiple_of(i * step_rows, step_rows), step_rows)
        v, t = act[at, :], bend[at, :]
        act[at, :] = 0.5 * (1.0 + t) + (0.5 * root) * v * (1.0 - t * t) * (
            1.0 + (3.0 * 0.044715) * (v * v)
        )


    for copy in rows_copies:
        copy.wait_recv()
    from_donor = jnp.concatenate([rows_in[h, 0:CAP, :] for h in range(HOPS)], axis=0)
    from_acceptor = jnp.concatenate(
        [rows_in[HOPS - 1 - h, CAP : 2 * CAP, :] for h in range(HOPS)], axis=0
    )
    other = jnp.concatenate([from_donor, dot(unchosen, from_acceptor).astype(BF16)], axis=0)
    other_f = other.astype(F32)
    pair = (own_rows.astype(F32) * other_f).astype(BF16)
    raw = dot(pair, scale[...], 1, 1) * inv_root
    small = jnp.exp(-jnp.abs(raw))
    sigmoid = jnp.where(raw >= 0.0, 1.0, small) / (1.0 + small)
    all_cot = jnp.concatenate([in_cot, cot[...].astype(F32) * live_col], axis=0)
    slope = (all_cot * sigmoid).astype(BF16)
    tissue = dot(slope[BUCKET:].T, pair[BUCKET:]) * inv_root
    tissue = jnp.concatenate([tissue, jnp.zeros((HEAD_PAD - TRACKS, CH), F32)], axis=0)
    for k in range(2):
        head[k] = tissue[:, k * HALF : (k + 1) * HALF]
        head_cast[k] = head[k].astype(BF16)
    head_copy = remote(head_cast.at[1 - core], head_in, S_HEAD, partner)
    start(head_copy)
    terms = dot(slope, scale[...]) * other_f * inv_root
    junction = dot(spread, terms.astype(BF16))
    for k in range(2):
        cols = slice(k * HALF, (k + 1) * HALF)
        total = fcot[:, cols].astype(F32) + junction[:, cols]
        pre[k] = (total * act[:, cols]).astype(BF16)
    pre_copy = remote(pre.at[1 - core], pre_in, S_PRE, partner)
    start(pre_copy)

    head_copy.wait_recv()
    head[core] = head[core] + head_in[...].astype(F32)
    for k in range(NX):
        base = (187 * k) // 4
        xt_out[k] = head[core, base : base + TROWS, :].astype(BF16)
    xt_copies = {}
    for step in X_FAR:
        to = wrapped(x + step, NX)
        xt_copies[step] = remote(
            xt_out.at[to], xt_in.at[step - 1], S_XT + step - 1, along_x(step)
        )
        start(xt_copies[step])

    smooth_copy.wait_recv()
    pre_copy.wait_recv()
    pre_own = pre[core]
    pre_other = pre_in[...]
    xm_copies = {}
    for n, piece in enumerate(PIECES):
        order = [wrapped(x + step, NX) for step in (*X_FAR, 0)]
        parts = [
            jnp.concatenate(
                [source[to, wrapped(z + step, NZ)] for to in order for step in piece], axis=0
            )
            for source in (smooth, smooth_in)
        ]
        block = dot(parts[0], pre_own) + dot(parts[1], pre_other)
        for k, step in enumerate(X_FAR):
            xm_out[n, step - 1] = block[k * PROWS : (k + 1) * PROWS].astype(BF16)
            copy = remote(
                xm_out.at[n, step - 1],
                xm_in.at[n, step - 1],
                S_XM + n * (NX - 1) + step - 1,
                along_x(step),
            )
            start(copy)
            xm_copies[n, step] = copy
        xm_own[n] = block[(NX - 1) * PROWS :]

    for step in X_NEAR:
        xt_copies[step].wait_recv()
    tail = xt_out[x].astype(F32)
    for step in range(1, NX):
        tail = tail + xt_in[step - 1].astype(F32)
    tail = tail.astype(BF16)
    stacked = jnp.concatenate([tail[:, k * 128 : (k + 1) * 128] for k in range(3)], axis=0)
    chunks = dot(z_pick, stacked).astype(BF16)
    for k in range(NZ):
        t_out[k] = chunks[k * ZROWS : (k + 1) * ZROWS]

    def t_copy(step):
        return remote(
            t_out.at[wrapped(z + step, NZ)], t_in.at[step - 1], S_T + step - 1, along_z(step)
        )

    t_copies = {step: t_copy(step) for step in range(1, NZ)}
    for step in Z_FAR:
        start(t_copies[step])

    z_copies = {}

    def pass_on(n):
        total = xm_own[n]
        for step in X_NEAR:
            xm_copies[n, step].wait_recv()
            total = total + xm_in[n, step - 1].astype(F32)
        for k, step in enumerate(PIECES[n]):
            rows = total[k * ZROWS : (k + 1) * ZROWS]
            if step == 0:
                z_own[...] = rows
                continue
            z_out[step - 1] = rows.astype(BF16)
            z_copies[step] = remote(
                z_out.at[step - 1], z_in.at[step - 1], S_Z + step - 1, along_z(step)
            )
            start(z_copies[step])

    pass_on(0)

    slope_s = dot(pre[0], mix[:, :HALF], 1, 1) + dot(pre[1], mix[:, HALF:], 1, 1)
    slope_s = slope_s.astype(BF16)
    spad[8 : 8 + ROWS, :] = slope_s.astype(F32)
    edge_out[0] = slope_s[ROWS - 16 :]
    edge_out[1] = slope_s[:16]
    edge_right = remote(edge_out.at[0], edge_in.at[0], S_SLOPE, along_seq(1))
    edge_left = remote(edge_out.at[1], edge_in.at[1], S_SLOPE + 1, along_seq(-1))
    start(edge_right)
    start(edge_left)

    depth = []
    for k in range(3):
        part = jnp.zeros((1, CH), F32)
        for at in range(0, ROWS, step_rows):
            part = part + jnp.sum(
                fpad[at + 7 + k : at + 7 + k + step_rows, :]
                * spad[at + 8 : at + 8 + step_rows, :],
                axis=0,
                keepdims=True,
            )
        depth.append(part * grad_scale)
    for k in range(2):
        lines = [
            depth[tap_at][:, k * HALF + tile * 128 : k * HALF + tile * 128 + 128]
            for tile in range(3)
            for tap_at in range(3)
        ]
        total = jnp.concatenate(lines + [jnp.zeros((16 - 9, 128), F32)], axis=0)
        taps_part[k] = total
        taps_cast[k] = total.astype(BF16)
    taps_copy = remote(taps_cast.at[1 - core], taps_in, S_TAPS, partner)
    start(taps_copy)

    pass_on(1)

    taps_copy.wait_recv()
    taps_sum[...] = taps_part[core] + taps_in[...].astype(F32)
    last_x, last_z = x == NX - 1, (x == NX - 1) & (z == NZ - 1)

    def taps_to_x(source):
        return remote(
            taps_out,
            taps_x.at[source],
            S_TAPS_X + source,
            {"seq": (NX - 1) * NZ + z, "dp": dp},
        )

    def taps_to_z(source):
        return remote(
            taps_out,
            taps_z.at[source],
            S_TAPS_Z + source,
            {"seq": NX * NZ - 1, "dp": dp},
        )

    for source in range(NX - 1):

        @pl.when(x == source)
        def _():
            taps_out[...] = taps_sum[...].astype(BF16)
            taps_to_x(source).start()

    pass_on(2)

    @pl.when(last_x)
    def _():
        total = taps_sum[...]
        for source in range(NX - 1):
            taps_to_x(source).wait_recv()
            total = total + taps_x[source].astype(F32)
        taps_sum[...] = total
        taps_out[...] = total.astype(BF16)

    for source in range(NZ - 1):

        @pl.when(last_x & (z == source))
        def _():
            taps_to_z(source).start()

    edge_right.wait_recv()
    edge_left.wait_recv()
    spad[0:8, :] = edge_in[0].astype(F32)[8:16] * inner_low
    spad[8 + ROWS : 16 + ROWS, :] = edge_in[1].astype(F32)[0:8] * inner_high
    for at in range(0, ROWS, step_rows):
        total = spad[at + 9 : at + 9 + step_rows, :] * tap[0]
        total = total + spad[at + 8 : at + 8 + step_rows, :] * tap[1]
        total = total + spad[at + 7 : at + 7 + step_rows, :] * tap[2]
        grad_out[at : at + step_rows, :] = total.astype(BF16)
    raw_d = raw[BUCKET:]
    softplus = jnp.maximum(raw_d, 0.0) + jnp.log1p(small[BUCKET:])
    scores_out[...] = softplus * live_col
    stores[0].start()
    stores[1].start()

    tail = t_out[z].astype(F32)
    for step in Z_FAR[::-1]:
        t_copies[step].wait_recv()
        tail = tail + t_in[step - 1].astype(F32)
    tail_sum[...] = tail

    @pl.when(last_z)
    def _():
        total = taps_sum[...]
        for source in range(NZ - 1):
            taps_to_z(source).wait_recv()
            total = total + taps_z[source].astype(F32)
        for tile in range(3):
            at = 5 * tile + 1
            tail_sum[at : at + 3, :] = tail_sum[at : at + 3, :] + total[3 * tile : 3 * tile + 3]

    total = z_own[...]
    for step in Z_FAR[::-1]:
        z_copies[step].wait_recv()
        total = total + z_in[step - 1].astype(F32)
    total = jnp.concatenate([total, tail_sum[...]], axis=1).astype(BF16)
    stacked = jnp.concatenate([total[:, k * 128 : (k + 1) * 128] for k in range(4)], axis=0)
    chunks = dot(d_pick, stacked).astype(BF16)
    for k in range(DP):
        d_out[k] = chunks[k * 16 : (k + 1) * 16]

    def d_copy(step):
        return remote(
            d_out.at[wrapped(dp + step, DP)], d_in.at[step - 1], S_Y + step - 1, along_dp(step)
        )

    d_copies = {step: d_copy(step) for step in range(1, DP)}
    for step in D_FAR:
        start(d_copies[step])
    sums = [d_out[dp].astype(F32), jnp.zeros((16, 128), F32)]
    for step in D_FAR[::-1]:
        d_copies[step].wait_recv()
        sums[step % 2] = sums[step % 2] + d_in[step - 1].astype(F32)

    first = core == 0
    low = jnp.where(first, sums[0], sums[1])
    high = jnp.where(first, sums[1], sums[0])

    def strip(source, base):
        return [source[base + k : base + k + 1, :] for k in range(3)]

    conv_out[...] = jnp.concatenate(strip(low, 0) + strip(high, 0), axis=1) * grad_scale
    stores[2].start()
    line = jnp.concatenate(
        strip(low, 3) + strip(high, 3) + strip(low, 6) + strip(high, 6), axis=1
    )
    number = seq * NY + y
    begin = number * (2 * SHARE) - lax.div(number * (2 * SHARE), CH) * CH + core * SHARE
    line = jnp.broadcast_to(line, (8, 2 * CH))
    line = pltpu.roll(line, lax.rem(2 * CH - begin, 2 * CH), 1)
    head_out[...] = line[0:1, :SHARE]
    stores[3].start()

    done()
    for source in range(NX - 1):

        @pl.when(x == source)
        def _():
            taps_to_x(source).wait_send()

    for source in range(NZ - 1):

        @pl.when(last_x & (z == source))
        def _():
            taps_to_z(source).wait_send()


def hand_over(*refs):
    sources, targets, held, sems = refs[:4], refs[4:8], refs[8:12], refs[12]
    loads = [
        pltpu.make_async_copy(src, dst, sems.at[k])
        for k, (src, dst) in enumerate(zip(sources, held))
    ]
    held = [held[0], held[1], held[2].at[0], held[3]]
    stores = [
        pltpu.make_async_copy(src, dst, sems.at[4 + k])
        for k, (src, dst) in enumerate(zip(held, targets))
    ]
    for copy in loads:
        copy.start()
    for load, store in zip(loads, stores):
        load.wait()
        store.start()
    for copy in stores:
        copy.wait()


def on_device(
    features,
    feature_cot,
    depth_weight,
    mix_weight,
    tissue_scale,
    donor_site,
    acceptor_hop,
    acceptor_site,
    live_count,
    score_cot,
):
    vmem = pl.BlockSpec(memory_space=pltpu.VMEM)
    hbm = pl.BlockSpec(memory_space=pltpu.HBM)

    def room(*shape, dtype=BF16):
        return pltpu.VMEM(shape, dtype)

    results = (
        jax.ShapeDtypeStruct((SLOTS, TRACKS), F32),
        jax.ShapeDtypeStruct((ROWS, CH), BF16),
        jax.ShapeDtypeStruct((1, CH), F32),
        jax.ShapeDtypeStruct((1, SHARE), F32),
    )
    made = pl.pallas_call(
        body,
        out_shape=results,
        in_specs=[hbm] * 10,
        out_specs=(hbm,) * 4,
        scratch_shapes=[
            room(SLOTS, TRACKS, dtype=F32),
            room(ROWS, CH),
            room(1, CH, dtype=F32),
            room(1, SHARE, dtype=F32),
            room(HOPS, CAP, 384),
            room(HOPS, CAP, 384),
            room(HOPS, 2 * CAP, CH),
            room(HOPS, 2 * CAP, CH),
            room(2, 16, CH),
            room(2, 16, CH),
            room(2, 16, CH),
            room(ROWS + 16, CH, dtype=F32),
            room(ROWS + 16, CH, dtype=F32),
            room(ROWS, CH, dtype=F32),
            room(ROWS, CH, dtype=F32),
            room(ROWS, CH),
            room(ROWS, CH),
            room(NX, NZ, ZROWS, ROWS),
            room(NX, NZ, ZROWS, ROWS),
            room(2, ROWS, HALF),
            room(ROWS, HALF),
            room(2, HEAD_PAD, HALF, dtype=F32),
            room(2, HEAD_PAD, HALF),
            room(HEAD_PAD, HALF),
            room(len(PIECES), NX - 1, PROWS, HALF),
            room(len(PIECES), PROWS, HALF, dtype=F32),
            room(len(PIECES), NX - 1, PROWS, HALF),
            room(NX, TROWS, HALF),
            room(NX - 1, TROWS, HALF),
            room(NZ - 1, ZROWS, HALF),
            room(ZROWS, HALF, dtype=F32),
            room(NZ - 1, ZROWS, HALF),
            room(NZ, ZROWS, 128),
            room(NZ - 1, ZROWS, 128),
            room(16, 128, dtype=F32),
            room(2, 16, 128, dtype=F32),
            room(2, 16, 128),
            room(16, 128),
            room(16, 128, dtype=F32),
            room(16, 128),
            room(NX - 1, 16, 128),
            room(NZ - 1, 16, 128),
            room(DP, 16, 128),
            room(DP - 1, 16, 128),
            pltpu.SemaphoreType.DMA((S_ALL,)),
            pltpu.SemaphoreType.DMA((S_ALL,)),
            room(ROWS, CH),
            room(ROWS, CH),
            room(3, CH),
            room(CH, CH),
            room(TRACKS, CH),
            room(1, SLOTS, dtype=jnp.int32),
            room(1, SLOTS, dtype=jnp.int32),
            room(1, SLOTS, dtype=jnp.int32),
            room(1, 1, dtype=jnp.int32),
            room(SLOTS, TRACKS),
            pltpu.SemaphoreType.DMA((14,)),
        ],
        compiler_params=pltpu.CompilerParams(
            collective_id=0, has_side_effects=True, vmem_limit_bytes=63 * 1024 * 1024
        ),
    )(
        features[0],
        feature_cot[0],
        depth_weight,
        mix_weight,
        tissue_scale,
        donor_site,
        acceptor_hop.reshape(1, SLOTS),
        acceptor_site,
        live_count,
        score_cot[0].T,
    )
    scores, grad, conv, head = pl.pallas_call(
        hand_over,
        out_shape=results[:2] + (jax.ShapeDtypeStruct((CH,), F32), results[3]),
        in_specs=[hbm] * 4,
        out_specs=(hbm,) * 4,
        scratch_shapes=[
            room(SLOTS, TRACKS, dtype=F32),
            room(ROWS, CH),
            room(1, CH, dtype=F32),
            room(1, SHARE, dtype=F32),
            pltpu.SemaphoreType.DMA((8,)),
        ],
        compiler_params=pltpu.CompilerParams(vmem_limit_bytes=63 * 1024 * 1024),
    )(*made)
    return scores.T[None], grad[None], conv, head.reshape(SHARE)


def solution(mesh):
    placed = (
        P("dp", "seq", None),
        P("dp", "seq", None),
        P(),
        P(),
        P(),
        P("dp", "seq"),
        P("dp", "seq", None),
        P("dp", "seq"),
        P("dp", "seq"),
        P("dp", None, "seq"),
    )
    return jax.shard_map(
        on_device,
        mesh=mesh,
        in_specs=placed,
        out_specs=(P("dp", None, "seq"), P("dp", "seq", None), P(("seq", "dp")), P(("seq", "dp"))),
        check_vma=False,
    )
```
